32 devices in a mesh: shard: 32 (over z, y, x, core), rep: 1.
Axes of the slice: x: 2, y: 2, z: 4, core: 2. Of those that a mesh axis runs over, the one named last changes fastest.
Arguments:
- queries: bfloat16 [128, 32, 128], P(('rep', 'shard')), may hold values from -6 to 6
- passages: bfloat16 [128, 128, 128], P(('shard', 'rep')), may hold values from -0.52734375 to 0.52734375
- labels: int32 [128, 128], P('shard'), may hold values from 0 to 9
- lengths: int32 [128], P('shard'), may hold values from 16 to 128
- candidates: int32 [128, 64], P(('rep', 'shard')), may hold values from 0 to 127, all different within a row
- feedback: int32 [128, 3], P('rep'), may hold values from 0 to 127
- idf: int32 [128, 10], P('rep'), may hold values from 1 to 16
Outputs:
- first_scores: float32 [128, 64], P(('rep', 'shard'))
- final_scores: float32 [128, 64], P(('rep', 'shard'))
The draws below stay inside these ranges and needn't reach their ends.
Inputs may be any that keep to these rules, and one draw needn't show every extreme that they name: `candidates`: each row names 64 different passages; every passage is named by some row. `feedback`: ids may repeat within a row.
All inputs are finite; a program needn't handle non-finite values.
Results may differ from the reference program's by a relative error of at most 0.0003.
Values may be sent and summed in bfloat16 or wider, within the bound.
No kernel may reach another device: no remote copies, remote signals or barrier semaphores. Data moves between devices by JAX's collectives and lax.ppermute only.
A program may use at most 64 MiB of HBM per device.

```python
import jax
import jax.numpy as jnp
from jax import lax

D = 128
QTOK = 32
PTOK = 128
NCLUS = 10
FB = 3
QUERIES = 128
PASSAGES = 128
NCAND = 64


def draw_lengths(key, part):
    drawn = jax.random.randint(key, (PASSAGES,), PTOK // 8, PTOK + 1, dtype=jnp.int32)
    drawn = drawn.at[0].set(PTOK)
    return drawn.at[1].set(PTOK // 8)


def set_ends(values, stream_key, low, high):
    spot = [jax.random.randint(jax.random.fold_in(stream_key, axis), (), 0, length) for axis, length in enumerate(values.shape)]
    widest = values.shape.index(max(values.shape))
    neighbour = spot[:widest] + [(spot[widest] + 1) % values.shape[widest]] + spot[widest + 1:]
    return values.at[tuple(spot)].set(low).at[tuple(neighbour)].set(high)


def block_levels(rng, shape, pieces, least, high):
    def one(dim, parts):
        steps = jax.random.uniform(jax.random.fold_in(jax.random.fold_in(rng, 6), dim), (parts,), jnp.float32, least / len(pieces), high / len(pieces))
        return jnp.repeat(jnp.exp(steps), shape[dim] // parts).reshape((-1,) + (1,) * (len(shape) - dim - 1))

    loudness = one(*pieces[0])
    for cut in pieces[1:]:
        loudness = loudness * one(*cut)
    return loudness


def choose_distinct(own_key, rows, amount, top, lift):
    ranking = jax.random.permutation(jax.random.fold_in(own_key, 1), amount)
    favour = ranking
    for power in range(3):
        favour = favour * favour // amount
    favour = favour * lift // amount
    chance = jax.random.randint(jax.random.fold_in(own_key, 2), (rows, amount), 0, 4096) + favour
    sure = jax.random.permutation(jax.random.fold_in(own_key, 3), rows)[jnp.arange(amount) % rows]
    chance = jnp.where(jnp.arange(rows)[:, None] == sure[None, :], 1 << 14, chance)
    merit = chance * amount + jnp.arange(amount)
    return lax.top_k(merit.astype(jnp.int32), top)[1].astype(jnp.int32)


def bell_draw(key, dims, spread, reach, cuts=(), kind=jnp.bfloat16):
    result = jax.random.normal(key, dims, jnp.float32) * spread
    if len(cuts) > 0:
        result = block_levels(key, dims, cuts, -0.22, 0.18) * result
    return jnp.clip(result, min=-reach, max=reach).astype(kind)


def setup_inputs(seed: int = 0) -> dict:
    seeds = jax.random.split(jax.random.key(seed), 8)
    queries = bell_draw(seeds[0], (QUERIES, QTOK, D), 1.0, 6.0, ((0, 32),))
    passages = bell_draw(seeds[1], (PASSAGES, PTOK, D), 0.0884, 0.52734375, ((0, 32),))
    labels = set_ends(jax.random.randint(seeds[2], (PASSAGES, PTOK), 0, NCLUS), jax.random.fold_in(seeds[2], 1), 0, NCLUS - 1).astype(jnp.int32)
    lengths = draw_lengths(jax.random.fold_in(seeds[7], 71), 0)
    candidates = choose_distinct(seeds[4], QUERIES, PASSAGES, NCAND, 8192)
    feedback = set_ends(jax.random.randint(seeds[5], (QUERIES, FB), 0, PASSAGES), jax.random.fold_in(seeds[5], 1), 0, PASSAGES - 1).astype(jnp.int32)
    idf = set_ends(jax.random.randint(seeds[6], (QUERIES, NCLUS), 1, 17), jax.random.fold_in(seeds[6], 1), 1, 16).astype(jnp.int32)
    return {"queries": queries, "passages": passages, "labels": labels, "lengths": lengths, "candidates": candidates, "feedback": feedback, "idf": idf}


def cluster_totals(passages, labels, lengths):
    positions = jnp.arange(PTOK, dtype=jnp.int32)
    in_length = positions[None, :] < lengths[:, None]
    clusters = jnp.arange(NCLUS, dtype=jnp.int32)
    one_hot = ((labels[:, :, None] == clusters[None, None, :]) & in_length[:, :, None]).astype(jnp.float32)
    return jnp.einsum('ptc,ptd->pcd', one_hot, passages.astype(jnp.float32), precision=lax.Precision.HIGHEST)

def normalize(pooled):
    factor = lax.rsqrt(lax.optimization_barrier(jnp.mean(pooled * pooled, axis=-1, keepdims=True)) + 1e-06)
    return (pooled * factor).astype(jnp.bfloat16)

def reference(queries, passages, labels, lengths, candidates, feedback, idf):
    totals = cluster_totals(passages, labels, lengths)
    pooled = lax.optimization_barrier(jnp.sum(jnp.take(totals, feedback, axis=0), axis=1))
    expansion = normalize(pooled)
    weights = idf.astype(jnp.float32) / (8.0 * NCLUS)
    positions = jnp.arange(PTOK, dtype=jnp.int32)

    def one_query(operand):
        query_vectors, expanded_rows, weight_row, candidate_ids = operand
        documents = jnp.take(passages, candidate_ids, axis=0).astype(jnp.float32)
        in_length = positions[None, :] < jnp.take(lengths, candidate_ids, axis=0)[:, None]
        combined = jnp.concatenate([query_vectors, expanded_rows], axis=0).astype(jnp.float32)
        scores = jnp.einsum('id,ktd->kit', combined, documents, precision=lax.Precision.HIGHEST)
        best_scores = lax.optimization_barrier(jnp.max(jnp.where(in_length[:, None, :], scores, -1000000000.0), axis=-1))
        plain_score = lax.optimization_barrier(jnp.mean(best_scores[:, :QTOK], axis=1))
        added_score = lax.optimization_barrier(jnp.sum(best_scores[:, QTOK:] * weight_row[None, :], axis=1))
        return (plain_score, plain_score + added_score)
    first_scores, final_scores = lax.map(one_query, (queries, expansion, weights, candidates))
    return (first_scores, final_scores)
```

```python
import functools

import jax
import jax.numpy as jnp
import numpy as np
from jax import lax
from jax.experimental import pallas as pl
from jax.experimental.pallas import tpu as pltpu
from jax.sharding import PartitionSpec as P

BANK_BITS = 3
HIGHEST = lax.Precision.HIGHEST
BF16, F32, I32 = jnp.bfloat16, jnp.float32, jnp.int32
VMEM_BYTES = 48 * 1024 * 1024


def iota(shape, dim):
    return lax.broadcasted_iota(I32, shape, dim)


def rows_dot(a, b, precision=None):
    return lax.dot_general(a, b, (((1,), (1,)), ((), ())), precision=precision, preferred_element_type=F32)


def prepare_kernel(clusters, lengths_ref, queries_ref, passages_ref, labels_ref, payload_ref, masked_ref):
    count, tokens, features = passages_ref.shape
    query_rows = queries_ref.shape[0]
    payload_ref[:query_rows, :] = queries_ref[...]
    totals = jnp.zeros((clusters * count, features), F32)
    for p in range(count):
        length = lengths_ref[p]
        document = passages_ref[p]
        wide = document.astype(F32)
        kept = jnp.where(iota((tokens, features), 0) < length, wide, wide[0:1, :])
        masked_ref[p * tokens : (p + 1) * tokens, :] = kept.astype(BF16)
        target = jnp.where(iota((1, tokens), 1) < length, labels_ref[p : p + 1, :] * count + p, -1)
        chosen = (iota((clusters * count, tokens), 0) == target).astype(F32).astype(BF16)
        totals = totals + jnp.dot(chosen, document, preferred_element_type=F32)
    high = totals.astype(BF16).astype(F32)
    payload_ref[query_rows:, :] = jnp.concatenate([high, totals - high], axis=0).astype(BF16)


def best_rows(document_refs, vectors, count):
    best = []
    for document_ref in document_refs:
        scores = rows_dot(document_ref[...], vectors)
        tokens = scores.shape[0] // count
        best += [jnp.max(scores[p * tokens : (p + 1) * tokens, :], axis=0, keepdims=True) for p in range(count)]
    return jnp.concatenate(best, axis=0)


def plain_kernel(count, query_tokens, query_rows, gathered_ref, *refs):
    document_refs, plain_ref = refs[:-1], refs[-1]
    slots = gathered_ref.shape[0]
    vectors = jnp.concatenate([gathered_ref[s, :query_rows, :] for s in range(slots)], axis=0)
    best = best_rows(document_refs, vectors, count)
    number = plain_ref.shape[0]
    shape = (number, vectors.shape[0])
    first = iota(shape, 0) * query_tokens
    mean = jnp.where((iota(shape, 1) >= first) & (iota(shape, 1) < first + query_tokens), 1.0 / query_tokens, 0.0)
    plain_ref[...] = rows_dot(mean.astype(F32), best, HIGHEST)


def expand_kernel(
    count, near_ref, far_ref, places_ref, feedback_ref, idf_ref, plain_ref, *refs, outputs, step
):
    document_refs, out_refs, fb_ref, weight_ref = refs[: -outputs - 2], refs[-outputs - 2 : -2], refs[-2], refs[-1]
    me = lax.axis_index("shard")
    number, clusters = weight_ref.shape
    each = number // outputs
    for s in range(outputs):
        base = (me ^ (s * step)) * each
        fb_ref[s * each : (s + 1) * each, :] = feedback_ref[pl.ds(base, each), :]
        weight_ref[s * each : (s + 1) * each, :] = idf_ref[pl.ds(base, each), :].astype(F32) / (8.0 * clusters)
    wanted = fb_ref[...] ^ (me * count)
    pooled = jnp.zeros((clusters * number, near_ref.shape[1]), F32)
    for half, totals_ref in enumerate((near_ref, far_ref)):
        place = places_ref[2 * half : 2 * half + 1, :]
        kind = places_ref[2 * half + 1 : 2 * half + 2, :]
        times = jnp.zeros((number, place.shape[1]), F32)
        for k in range(wanted.shape[1]):
            times = times + jnp.where(wanted[:, k : k + 1] == place, 1.0, 0.0)
        picks = jnp.concatenate([jnp.where(kind == c, times, 0.0) for c in range(clusters)], axis=0)
        pooled = pooled + jnp.dot(picks.astype(BF16), totals_ref[...], preferred_element_type=F32)
    factor = lax.rsqrt(jnp.mean(pooled * pooled, axis=-1, keepdims=True) + 1e-06)
    expansion = (pooled * factor).astype(BF16)
    best = best_rows(document_refs, expansion, count)
    shape = (number, clusters * number)
    spread = jnp.zeros(shape, F32)
    for c in range(clusters):
        spread = jnp.where(iota(shape, 1) == iota(shape, 0) + c * number, weight_ref[:, c : c + 1], spread)
    added = rows_dot(spread, best, HIGHEST)
    plain = plain_ref[...]
    both = jnp.concatenate([plain, plain + added], axis=1)
    for s in range(outputs):
        out_refs[s][...] = both[s * each : (s + 1) * each, :]


def select_kernel(count, candidates_ref, *refs):
    block_refs, first_ref, final_ref = refs[:-2], refs[-2], refs[-1]
    me = lax.axis_index("shard")
    given, wanted = candidates_ref.shape
    width = block_refs[0].shape[1] // 2
    place = candidates_ref[...] ^ (me * count)
    rows, lanes = -(-given // 8) * 8, -(-wanted // 128) * 128
    place = jnp.pad(place, ((0, rows - given), (0, lanes - wanted)))
    for side, out_ref in enumerate((first_ref, final_ref)):
        dense = jnp.concatenate([r[:, side * width : (side + 1) * width] for r in block_refs], axis=1)
        dense = jnp.pad(dense, ((0, rows - given), (0, 0)))
        pieces = []
        for at in range(0, place.shape[1], 128):
            here = place[:, at : at + 128]
            piece = jnp.zeros((rows, 128), F32)
            for group in range(dense.shape[1] // 128):
                found = jnp.take_along_axis(
                    dense[:, group * 128 : (group + 1) * 128], here & 127, axis=1, mode="promise_in_bounds"
                )
                piece = jnp.where((here >> 7) == group, found, piece)
            pieces.append(piece)
        out_ref[...] = jnp.concatenate(pieces, axis=1)[:given, :wanted]


def call(kernel, out_shape, *operands, scratch=(), specs=None, cost=None):
    return pl.pallas_call(
        kernel,
        out_shape=out_shape,
        in_specs=specs or [pl.BlockSpec(memory_space=pltpu.VMEM)] * len(operands),
        scratch_shapes=scratch,
        compiler_params=pltpu.CompilerParams(vmem_limit_bytes=VMEM_BYTES),
        cost_estimate=cost,
    )(*operands)


def local(devices, queries, passages, labels, lengths, candidates, feedback, idf):
    passages = lax.all_gather(passages, "rep", axis=0, tiled=True)
    count, tokens, features = passages.shape
    each, query_tokens, _ = queries.shape
    clusters = idf.shape[1]
    bank = min(1 << BANK_BITS, devices)
    columns = devices // bank
    number = columns * each
    query_rows = each * query_tokens
    total_rows = 2 * clusters * count
    sds = jax.ShapeDtypeStruct

    def swap(x, m):
        return lax.ppermute(x, "shard", [(i, i ^ m) for i in range(devices)])

    vmem, smem = pl.BlockSpec(memory_space=pltpu.VMEM), pl.BlockSpec(memory_space=pltpu.SMEM)
    payload, masked = call(
        functools.partial(prepare_kernel, clusters),
        (sds((query_rows + total_rows, features), BF16), sds((count * tokens, features), BF16)),
        lengths,
        queries.reshape(query_rows, features),
        passages,
        labels,
        specs=[smem, vmem, vmem, vmem],
    )
    gathered = payload[None]
    for bit in range(columns.bit_length() - 1):
        gathered = jnp.concatenate([gathered, swap(gathered, bank << bit)], axis=0)
    documents = {0: masked}
    for m in range(2, bank, 2):
        documents[m] = swap(masked, m)
    for m in range(0, bank, 2):
        documents[m + 1] = swap(documents[m], 1)
    documents = [documents[m] for m in range(bank)]
    own = gathered[:, query_rows:, :].reshape(columns * total_rows, features)
    near = jnp.concatenate([own] + [swap(own, m) for m in range(2, bank, 2)], axis=0)
    far = swap(near, 1)
    plain = call(
        functools.partial(plain_kernel, count, query_tokens, query_rows),
        sds((number, bank * count), F32),
        gathered,
        *documents,
    )
    row = np.arange(total_rows) % (clusters * count)
    places = []
    for half in range(2):
        m = np.arange(half, bank, 2)[:, None, None]
        s = np.arange(columns)[None, :, None] * bank
        place = (m + s) * count + (row % count)[None, None, :]
        kind = np.broadcast_to((row // count)[None, None, :], place.shape)
        places += [place.reshape(-1), kind.reshape(-1)]
    blocks = call(
        functools.partial(expand_kernel, count, outputs=columns, step=bank),
        [sds((each, 2 * bank * count), F32)] * columns,
        near,
        far,
        jnp.asarray(np.stack(places).astype(np.int32)),
        feedback,
        idf,
        plain,
        *documents,
        scratch=[pltpu.VMEM((number, feedback.shape[1]), I32), pltpu.VMEM((number, clusters), F32)],
    )
    blocks = [blocks[0]] + [swap(blocks[s], s * bank) for s in range(1, columns)]
    return call(
        functools.partial(select_kernel, count),
        (sds(candidates.shape, F32), sds(candidates.shape, F32)),
        candidates,
        *blocks,
    )


def solution(mesh):
    return jax.shard_map(
        functools.partial(local, mesh.shape["shard"]),
        mesh=mesh,
        in_specs=(
            P(("rep", "shard"), None, None),
            P(("shard", "rep"), None, None),
            P("shard", None),
            P("shard"),
            P(("rep", "shard"), None),
            P("rep", None),
            P("rep", None),
        ),
        out_specs=(P(("rep", "shard"), None), P(("rep", "shard"), None)),
        check_vma=False,
    )
```

```python
import functools

import jax
import jax.numpy as jnp
import numpy as np
from jax import lax
from jax.experimental import pallas as pl
from jax.experimental.pallas import tpu as pltpu
from jax.sharding import PartitionSpec as P

BANK_BITS = 3
HIGHEST = lax.Precision.HIGHEST
BF16, F32, I32 = jnp.bfloat16, jnp.float32, jnp.int32
COST = 10**9
VMEM_BYTES = 48 * 1024 * 1024


def iota(shape, dim):
    return lax.broadcasted_iota(I32, shape, dim)


def rows_dot(a, b, precision=None):
    return lax.dot_general(a, b, (((1,), (1,)), ((), ())), precision=precision, preferred_element_type=F32)


def prepare_kernel(
    clusters, lengths_hbm, queries_hbm, passages_hbm, labels_hbm, payload_ref, masked_ref, lengths_ref, passages_ref, labels_ref, arrived
):
    query_rows = queries_hbm.shape[0]
    copies = [
        pltpu.make_async_copy(passages_hbm, passages_ref, arrived.at[0]),
        pltpu.make_async_copy(lengths_hbm, lengths_ref, arrived.at[1]),
        pltpu.make_async_copy(labels_hbm, labels_ref, arrived.at[2]),
        pltpu.make_async_copy(queries_hbm, payload_ref.at[:query_rows, :], arrived.at[3]),
    ]
    for copy in copies:
        copy.start()
    count, tokens, features = passages_ref.shape
    totals = jnp.zeros((clusters * count, features), F32)
    for copy in copies[:3]:
        copy.wait()
    for p in range(count):
        length = lengths_ref[0:1, p : p + 1]
        document = passages_ref[p]
        wide = document.astype(F32)
        kept = jnp.where(iota((tokens, features), 0) < length, wide, wide[0:1, :])
        masked_ref[p * tokens : (p + 1) * tokens, :] = kept.astype(BF16)
        target = jnp.where(iota((1, tokens), 1) < length, labels_ref[p : p + 1, :] * count + p, -1)
        chosen = (iota((clusters * count, tokens), 0) == target).astype(F32).astype(BF16)
        totals = totals + jnp.dot(chosen, document, preferred_element_type=F32)
    high = totals.astype(BF16).astype(F32)
    payload_ref[query_rows:, :] = jnp.concatenate([high, totals - high], axis=0).astype(BF16)
    copies[3].wait()


def best_rows(document_refs, vectors, count, tokens):
    best, rows = [], count * tokens
    for document_ref in document_refs:
        for at in range(0, document_ref.shape[0], rows):
            scores = rows_dot(document_ref[at : at + rows, :], vectors)
            best += [jnp.max(scores[p * tokens : (p + 1) * tokens, :], axis=0, keepdims=True) for p in range(count)]
    return jnp.concatenate(best, axis=0)


def plain_kernel(count, tokens, query_tokens, query_rows, early_ref, late_ref, *refs):
    document_refs, plain_ref = refs[:-1], refs[-1]
    vectors = jnp.concatenate([slot[:query_rows, :] for slot in slots_of((early_ref, late_ref))], axis=0)
    best = best_rows(document_refs, vectors, count, tokens)
    shape = (plain_ref.shape[0], vectors.shape[0])
    first = iota(shape, 0) * query_tokens
    mean = jnp.where((iota(shape, 1) >= first) & (iota(shape, 1) < first + query_tokens), 1.0 / query_tokens, 0.0)
    plain_ref[...] = rows_dot(mean.astype(F32), best, HIGHEST)


def picks_kernel(
    count, slots, step, places_ref, feedback_ref, idf_ref, near_ref, far_ref, spread_ref, fb_ref, weight_ref
):
    number, clusters = weight_ref.shape
    me = lax.axis_index("shard")
    each = number // slots
    for s in range(slots):
        base = (me ^ (s * step)) * each
        fb_ref[s * each : (s + 1) * each, :] = feedback_ref[pl.ds(base, each), :]
        weight_ref[s * each : (s + 1) * each, :] = idf_ref[pl.ds(base, each), :].astype(F32) / (8.0 * clusters)
    wanted = fb_ref[...] ^ (me * count)
    for half, picks_ref in enumerate((near_ref, far_ref)):
        place = places_ref[2 * half : 2 * half + 1, :]
        kind = places_ref[2 * half + 1 : 2 * half + 2, :]
        times = jnp.zeros((number, place.shape[1]), F32)
        for k in range(wanted.shape[1]):
            times = times + jnp.where(wanted[:, k : k + 1] == place, 1.0, 0.0)
        for c in range(clusters):
            picks_ref[c * number : (c + 1) * number, :] = jnp.where(kind == c, times, 0.0).astype(BF16)
    shape = (number, clusters * number)
    spread = jnp.zeros(shape, F32)
    for c in range(clusters):
        spread = jnp.where(iota(shape, 1) == iota(shape, 0) + c * number, weight_ref[:, c : c + 1], spread)
    spread_ref[...] = spread


def slots_of(refs):
    return [ref.at[s] for ref in refs for s in range(ref.shape[0])]


def totals_kernel(skip, early_ref, late_ref, totals_ref):
    slots = slots_of((early_ref, late_ref))
    rows = totals_ref.shape[0] // len(slots)
    for s, slot in enumerate(slots):
        totals_ref[s * rows : (s + 1) * rows, :] = slot[skip:, :]


def pool_kernel(picks_ref, totals_ref, pooled_ref):
    pooled_ref[...] = jnp.dot(picks_ref[...], totals_ref[...], preferred_element_type=F32)


def expand_kernel(
    count, tokens, outputs, near_pooled_ref, far_ref, far_picks_ref, spread_ref, near_plain_ref, far_plain_ref, *refs
):
    document_refs, out_refs = refs[:-outputs], refs[-outputs:]
    pooled = near_pooled_ref[...] + jnp.dot(far_picks_ref[...], far_ref[...], preferred_element_type=F32)
    factor = lax.rsqrt(jnp.mean(pooled * pooled, axis=-1, keepdims=True) + 1e-06)
    expansion = (pooled * factor).astype(BF16)
    best = best_rows(document_refs, expansion, count, tokens)
    added = rows_dot(spread_ref[...], best, HIGHEST)
    plain = jnp.concatenate([near_plain_ref[...], far_plain_ref[...]], axis=1)
    both = jnp.concatenate([plain, plain + added], axis=1)
    each = both.shape[0] // outputs
    for s in range(outputs):
        out_refs[s][...] = both[s * each : (s + 1) * each, :]


def select_kernel(count, candidates_ref, *refs):
    block_refs, first_ref, final_ref = refs[:-2], refs[-2], refs[-1]
    me = lax.axis_index("shard")
    given, wanted = candidates_ref.shape
    width = block_refs[0].shape[1] // 2
    place = candidates_ref[...] ^ (me * count)
    owner, within = place // count % (width // count), place % count
    half = width // 2
    place = place // width * width + (owner & 1) * half + (owner >> 1) * count + within
    rows, lanes = -(-given // 8) * 8, -(-wanted // 128) * 128
    place = jnp.pad(place, ((0, rows - given), (0, lanes - wanted)))
    for side, out_ref in enumerate((first_ref, final_ref)):
        dense = jnp.concatenate([r[:, side * width : (side + 1) * width] for r in block_refs], axis=1)
        dense = jnp.pad(dense, ((0, rows - given), (0, 0)))
        pieces = []
        for at in range(0, place.shape[1], 128):
            here = place[:, at : at + 128]
            piece = jnp.zeros((rows, 128), F32)
            for group in range(dense.shape[1] // 128):
                found = jnp.take_along_axis(
                    dense[:, group * 128 : (group + 1) * 128], here & 127, axis=1, mode="promise_in_bounds"
                )
                piece = jnp.where((here >> 7) == group, found, piece)
            pieces.append(piece)
        out_ref[...] = jnp.concatenate(pieces, axis=1)[:given, :wanted]


def call(kernel, out_shape, *operands, scratch=(), specs=None, cost=None, vmem=VMEM_BYTES):
    return pl.pallas_call(
        kernel,
        out_shape=out_shape,
        in_specs=specs or [pl.BlockSpec(memory_space=pltpu.VMEM)] * len(operands),
        scratch_shapes=scratch,
        compiler_params=pltpu.CompilerParams(vmem_limit_bytes=vmem),
        cost_estimate=cost,
    )(*operands)


def local(devices, queries, passages, labels, lengths, candidates, feedback, idf):
    passages = lax.all_gather(passages, "rep", axis=0, tiled=True)
    count, tokens, features = passages.shape
    each, query_tokens, _ = queries.shape
    clusters = idf.shape[1]
    bank = min(1 << BANK_BITS, devices)
    columns = devices // bank
    number = columns * each
    query_rows = each * query_tokens
    total_rows = 2 * clusters * count
    sds = jax.ShapeDtypeStruct

    def swap(x, m):
        return lax.ppermute(x, "shard", [(i, i ^ m) for i in range(devices)])

    payload, masked = call(
        functools.partial(prepare_kernel, clusters),
        (sds((query_rows + total_rows, features), BF16), sds((count * tokens, features), BF16)),
        *[
            pltpu.with_memory_space_constraint(x, pltpu.HBM)
            for x in (lengths.reshape(1, count), queries.reshape(query_rows, features), passages, labels)
        ],
        specs=[pl.BlockSpec(memory_space=pltpu.HBM)] * 4,
        scratch=[
            pltpu.VMEM((1, count), I32),
            pltpu.VMEM((count, tokens, features), BF16),
            pltpu.VMEM((count, tokens), I32),
            pltpu.SemaphoreType.DMA((4,)),
        ],
    )
    received = swap(payload[None], bank)
    received, masked = lax.optimization_barrier((received, masked))
    gathered = [payload[None], received]
    row = np.arange(total_rows) % (clusters * count)
    places = []
    for half in range(2):
        m = np.arange(half, bank, 2)[:, None, None]
        s = np.arange(columns)[None, :, None] * bank
        place = (m + s) * count + (row % count)[None, None, :]
        kind = np.broadcast_to((row // count)[None, None, :], place.shape)
        places += [place.reshape(-1), kind.reshape(-1)]
    places = jnp.asarray(np.stack(places).astype(np.int32))
    picks = call(
        functools.partial(picks_kernel, count, columns, bank),
        (
            sds((clusters * number, places.shape[1]), BF16),
            sds((clusters * number, places.shape[1]), BF16),
            sds((number, clusters * number), F32),
        ),
        places,
        feedback,
        idf,
        scratch=[pltpu.VMEM((number, feedback.shape[1]), I32), pltpu.VMEM((number, clusters), F32)],
    )
    for bit in range(1, columns.bit_length() - 1):
        early = jnp.concatenate(gathered, axis=0)
        gathered = [early, swap(early, bank << bit)]
    documents = [masked] + [swap(masked, m) for m in range(2, bank, 2)]
    far_documents = swap(jnp.concatenate(documents, axis=0), 1)
    half = bank * count // 2
    plain = functools.partial(plain_kernel, count, tokens, query_tokens, query_rows)
    near_plain = call(plain, sds((number, half), F32), *gathered, *documents)
    far_plain = call(plain, sds((number, half), F32), *gathered, far_documents)
    own = call(
        functools.partial(totals_kernel, query_rows),
        sds((columns * total_rows, features), BF16),
        *gathered,
        cost=pl.CostEstimate(flops=COST, bytes_accessed=0, transcendentals=0),
    )
    near_plain, picks, *others = lax.optimization_barrier((near_plain, picks, *[swap(own, m) for m in range(2, bank, 2)]))
    near = jnp.concatenate([own, *others], axis=0)
    far = swap(near, 1)
    near_picks, far_picks, spread = picks
    near_pooled = call(pool_kernel, sds((clusters * number, features), F32), near_picks, near)
    blocks = call(
        functools.partial(expand_kernel, count, tokens, columns),
        [sds((each, 2 * bank * count), F32)] * columns,
        near_pooled,
        far,
        far_picks,
        spread,
        near_plain,
        far_plain,
        *documents,
        far_documents,
    )
    blocks = [blocks[0]] + [swap(blocks[s], s * bank) for s in range(1, columns)]
    return call(
        functools.partial(select_kernel, count),
        (sds(candidates.shape, F32), sds(candidates.shape, F32)),
        candidates,
        *blocks,
    )


def solution(mesh):
    return jax.shard_map(
        functools.partial(local, mesh.shape["shard"]),
        mesh=mesh,
        in_specs=(
            P(("rep", "shard"), None, None),
            P(("shard", "rep"), None, None),
            P("shard", None),
            P("shard"),
            P(("rep", "shard"), None),
            P("rep", None),
            P("rep", None),
        ),
        out_specs=(P(("rep", "shard"), None), P(("rep", "shard"), None)),
        check_vma=False,
    )
```

```python
import functools

import jax
import jax.numpy as jnp
from jax import lax
from jax.experimental import pallas as pl
from jax.experimental.pallas import tpu as pltpu
from jax.sharding import PartitionSpec as P

BANK_BITS = 3
HIGHEST = lax.Precision.HIGHEST
BF16, F32, I32 = jnp.bfloat16, jnp.float32, jnp.int32
COST = 10**9
VMEM_BYTES = 48 * 1024 * 1024


def iota(shape, dim):
    return lax.broadcasted_iota(I32, shape, dim)


def rows_dot(a, b, precision=None):
    return lax.dot_general(a, b, (((1,), (1,)), ((), ())), precision=precision, preferred_element_type=F32)


def prepare_kernel(
    clusters, lengths_hbm, queries_hbm, passages_hbm, labels_hbm, payload_ref, masked_ref, lengths_ref, passages_ref, labels_ref, arrived
):
    query_rows = queries_hbm.shape[0]
    copies = [
        pltpu.make_async_copy(passages_hbm, passages_ref, arrived.at[0]),
        pltpu.make_async_copy(lengths_hbm, lengths_ref, arrived.at[1]),
        pltpu.make_async_copy(labels_hbm, labels_ref, arrived.at[2]),
        pltpu.make_async_copy(queries_hbm, payload_ref.at[:query_rows, :], arrived.at[3]),
    ]
    for copy in copies:
        copy.start()
    count, tokens, features = passages_ref.shape
    totals = jnp.zeros((clusters * count, features), F32)
    for copy in copies[:3]:
        copy.wait()
    for p in range(count):
        length = lengths_ref[0:1, p : p + 1]
        document = passages_ref[p]
        wide = document.astype(F32)
        kept = jnp.where(iota((tokens, features), 0) < length, wide, wide[0:1, :])
        masked_ref[p * tokens : (p + 1) * tokens, :] = kept.astype(BF16)
        target = jnp.where(iota((1, tokens), 1) < length, labels_ref[p : p + 1, :] * count + p, -1)
        chosen = (iota((clusters * count, tokens), 0) == target).astype(F32).astype(BF16)
        totals = totals + jnp.dot(chosen, document, preferred_element_type=F32)
    high = totals.astype(BF16).astype(F32)
    payload_ref[query_rows:, :] = jnp.concatenate([high, totals - high], axis=0).astype(BF16)
    copies[3].wait()


def best_rows(document_refs, vectors, count, tokens):
    best, rows = [], count * tokens
    for document_ref in document_refs:
        for at in range(0, document_ref.shape[0], rows):
            scores = rows_dot(document_ref[at : at + rows, :], vectors)
            best += [jnp.max(scores[p * tokens : (p + 1) * tokens, :], axis=0, keepdims=True) for p in range(count)]
    return jnp.concatenate(best, axis=0)


def plain_kernel(count, tokens, query_tokens, query_rows, slots, *refs):
    gathered_refs, document_refs, plain_ref = refs[:slots], refs[slots:-1], refs[-1]
    vectors = jnp.concatenate([slot[:query_rows, :] for slot in gathered_refs], axis=0)
    best = best_rows(document_refs, vectors, count, tokens)
    shape = (plain_ref.shape[0], vectors.shape[0])
    first = iota(shape, 0) * query_tokens
    mean = jnp.where((iota(shape, 1) >= first) & (iota(shape, 1) < first + query_tokens), 1.0 / query_tokens, 0.0)
    plain_ref[...] = rows_dot(mean.astype(F32), best, HIGHEST)


def parts(index, size):
    whole = jnp.floor((index.astype(F32) + 0.5) * (1.0 / size)).astype(I32)
    return whole, index - whole * size


def relative(passage, me, count, bank, columns):
    owner, within = passage // count, passage % count
    column = (owner // bank + columns - me // bank) % columns
    return (column * bank + (owner % bank ^ me % bank)) * count + within


def near_kernel(count, tokens, query_tokens, query_rows, bank, slots, feedback_ref, idf_ref, *refs):
    refs, (plain_ref, near_ref, far_ref, spread_ref, fb_ref, weight_ref) = refs[:-6], refs[-6:]
    plain_kernel(count, tokens, query_tokens, query_rows, len(slots), *refs, plain_ref)
    me = lax.axis_index("shard")
    number, clusters = weight_ref.shape
    each = number // len(slots)
    for s, slot in enumerate(slots):
        base = (me % bank + (me // bank + slot) % len(slots) * bank) * each
        fb_ref[s * each : (s + 1) * each, :] = feedback_ref[pl.ds(base, each), :]
        weight_ref[s * each : (s + 1) * each, :] = idf_ref[pl.ds(base, each), :].astype(F32) / (8.0 * clusters)
    wanted = relative(fb_ref[...], me, count, bank, len(slots))
    block, row = parts(iota((1, near_ref.shape[1]), 1), 2 * clusters * count)
    block, column = parts(block, len(slots))
    kind, within = parts(jnp.where(row < clusters * count, row, row - clusters * count), count)
    owner = 2 * block
    for s, slot in enumerate(slots):
        owner = jnp.where(column == s, owner + slot * bank, owner)
    for half, picks_ref in enumerate((near_ref, far_ref)):
        place = (owner ^ half) * count + within
        times = jnp.zeros((number, place.shape[1]), F32)
        for k in range(wanted.shape[1]):
            times = times + jnp.where(wanted[:, k : k + 1] == place, 1.0, 0.0)
        for c in range(clusters):
            picks_ref[c * number : (c + 1) * number, :] = jnp.where(kind == c, times, 0.0).astype(BF16)
    shape = (number, clusters * number)
    spread = jnp.zeros(shape, F32)
    for c in range(clusters):
        spread = jnp.where(iota(shape, 1) == iota(shape, 0) + c * number, weight_ref[:, c : c + 1], spread)
    spread_ref[...] = spread


def totals_kernel(skip, *refs):
    slots, totals_ref = refs[:-1], refs[-1]
    rows = totals_ref.shape[0] // len(slots)
    for s, slot in enumerate(slots):
        totals_ref[s * rows : (s + 1) * rows, :] = slot[skip:, :]


def pool_kernel(picks_ref, totals_ref, pooled_ref):
    pooled_ref[...] = jnp.dot(picks_ref[...], totals_ref[...], preferred_element_type=F32)


def expand_kernel(
    count, tokens, places, near_pooled_ref, far_ref, far_picks_ref, spread_ref, near_plain_ref, far_plain_ref, *refs
):
    outputs = len(places)
    document_refs, out_refs = refs[:-outputs], refs[-outputs:]
    pooled = near_pooled_ref[...] + jnp.dot(far_picks_ref[...], far_ref[...], preferred_element_type=F32)
    factor = lax.rsqrt(jnp.mean(pooled * pooled, axis=-1, keepdims=True) + 1e-06)
    expansion = (pooled * factor).astype(BF16)
    best = best_rows(document_refs, expansion, count, tokens)
    added = rows_dot(spread_ref[...], best, HIGHEST)
    plain = jnp.concatenate([near_plain_ref[...], far_plain_ref[...]], axis=1)
    both = jnp.concatenate([plain, plain + added], axis=1)
    each = both.shape[0] // outputs
    for place, out_ref in zip(places, out_refs):
        out_ref[...] = both[place * each : (place + 1) * each, :]


def select_kernel(count, bank, places, candidates_ref, *refs):
    block_refs, first_ref, final_ref = [refs[i] for i in places], refs[-2], refs[-1]
    me = lax.axis_index("shard")
    given, wanted = candidates_ref.shape
    width = block_refs[0].shape[1] // 2
    place = relative(candidates_ref[...], me, count, bank, len(places))
    owner, within = place // count % (width // count), place % count
    half = width // 2
    place = place // width * width + (owner & 1) * half + (owner >> 1) * count + within
    rows, lanes = -(-given // 8) * 8, -(-wanted // 128) * 128
    place = jnp.pad(place, ((0, rows - given), (0, lanes - wanted)))
    for side, out_ref in enumerate((first_ref, final_ref)):
        dense = jnp.concatenate([r[:, side * width : (side + 1) * width] for r in block_refs], axis=1)
        dense = jnp.pad(dense, ((0, rows - given), (0, 0)))
        pieces = []
        for at in range(0, place.shape[1], 128):
            here = place[:, at : at + 128]
            piece = jnp.zeros((rows, 128), F32)
            for group in range(dense.shape[1] // 128):
                found = jnp.take_along_axis(
                    dense[:, group * 128 : (group + 1) * 128], here & 127, axis=1, mode="promise_in_bounds"
                )
                piece = jnp.where((here >> 7) == group, found, piece)
            pieces.append(piece)
        out_ref[...] = jnp.concatenate(pieces, axis=1)[:given, :wanted]


def call(kernel, out_shape, *operands, scratch=(), specs=None, cost=None, vmem=VMEM_BYTES):
    return pl.pallas_call(
        kernel,
        out_shape=out_shape,
        in_specs=specs or [pl.BlockSpec(memory_space=pltpu.VMEM)] * len(operands),
        scratch_shapes=scratch,
        compiler_params=pltpu.CompilerParams(vmem_limit_bytes=vmem),
        cost_estimate=cost,
    )(*operands)


def local(devices, queries, passages, labels, lengths, candidates, feedback, idf):
    passages = lax.all_gather(passages, "rep", axis=0, tiled=True)
    count, tokens, features = passages.shape
    each, query_tokens, _ = queries.shape
    clusters = idf.shape[1]
    bank = min(1 << BANK_BITS, devices)
    columns = devices // bank
    number = columns * each
    query_rows = each * query_tokens
    total_rows = 2 * clusters * count
    sds = jax.ShapeDtypeStruct

    def shift(x, s):
        return lax.ppermute(x, "shard", [(i, (i + s * bank) % devices) for i in range(devices)])

    def swap(x, m):
        return lax.ppermute(x, "shard", [(i, i ^ m) for i in range(devices)])

    payload, masked = call(
        functools.partial(prepare_kernel, clusters),
        (sds((query_rows + total_rows, features), BF16), sds((count * tokens, features), BF16)),
        *[
            pltpu.with_memory_space_constraint(x, pltpu.HBM)
            for x in (lengths.reshape(1, count), queries.reshape(query_rows, features), passages, labels)
        ],
        specs=[pl.BlockSpec(memory_space=pltpu.HBM)] * 4,
        scratch=[
            pltpu.VMEM((1, count), I32),
            pltpu.VMEM((count, tokens, features), BF16),
            pltpu.VMEM((count, tokens), I32),
            pltpu.SemaphoreType.DMA((4,)),
        ],
    )
    slots = list(range(columns))
    gathered = [payload] + [shift(payload, -s) for s in slots[1:]]
    documents = [masked] + [swap(masked, m) for m in range(2, bank, 2)]
    far_documents = swap(jnp.concatenate(documents, axis=0), 1)
    half = bank * count // 2
    plain = functools.partial(plain_kernel, count, tokens, query_tokens, query_rows, columns)
    picks_shape = sds((clusters * number, bank // 2 * columns * total_rows), BF16)
    ready = call(
        functools.partial(near_kernel, count, tokens, query_tokens, query_rows, bank, slots),
        (sds((number, half), F32), picks_shape, picks_shape, sds((number, clusters * number), F32)),
        feedback,
        idf,
        *gathered,
        *documents,
        scratch=[pltpu.VMEM((number, feedback.shape[1]), I32), pltpu.VMEM((number, clusters), F32)],
    )
    far_plain = call(plain, sds((number, half), F32), *gathered, far_documents)
    own = call(
        functools.partial(totals_kernel, query_rows),
        sds((columns * total_rows, features), BF16),
        *gathered,
        cost=pl.CostEstimate(flops=COST, bytes_accessed=0, transcendentals=0),
    )
    ready, *others = lax.optimization_barrier((ready, *[swap(own, m) for m in range(2, bank, 2)]))
    near_plain, near_picks, far_picks, spread = ready
    near = jnp.concatenate([own, *others], axis=0)
    far = swap(near, 1)
    near_pooled = call(pool_kernel, sds((clusters * number, features), F32), near_picks, near)
    returns = slots[1:] + slots[:1]
    blocks = call(
        functools.partial(expand_kernel, count, tokens, [slots.index(m) for m in returns]),
        [sds((each, 2 * bank * count), F32)] * columns,
        near_pooled,
        far,
        far_picks,
        spread,
        near_plain,
        far_plain,
        *documents,
        far_documents,
    )
    blocks = [shift(block, s) if s else block for s, block in zip(returns, blocks)]
    return call(
        functools.partial(select_kernel, count, bank, [returns.index(-s % columns) for s in range(columns)]),
        (sds(candidates.shape, F32), sds(candidates.shape, F32)),
        candidates,
        *blocks,
    )


def solution(mesh):
    return jax.shard_map(
        functools.partial(local, mesh.shape["shard"]),
        mesh=mesh,
        in_specs=(
            P(("rep", "shard"), None, None),
            P(("shard", "rep"), None, None),
            P("shard", None),
            P("shard"),
            P(("rep", "shard"), None),
            P("rep", None),
            P("rep", None),
        ),
        out_specs=(P(("rep", "shard"), None), P(("rep", "shard"), None)),
        check_vma=False,
    )
```

```python
import functools

import jax
import jax.numpy as jnp
from jax import lax
from jax.experimental import pallas as pl
from jax.experimental.pallas import tpu as pltpu
from jax.sharding import PartitionSpec as P

BANK_BITS = 3
HIGHEST = lax.Precision.HIGHEST
BF16, F32, I32 = jnp.bfloat16, jnp.float32, jnp.int32
VMEM_BYTES = 48 * 1024 * 1024


def iota(shape, dim):
    return lax.broadcasted_iota(I32, shape, dim)


def rows_dot(a, b, precision=None):
    return lax.dot_general(a, b, (((1,), (1,)), ((), ())), precision=precision, preferred_element_type=F32)


def prepare_kernel(
    clusters, lengths_hbm, queries_hbm, passages_hbm, labels_hbm, payload_ref, masked_ref, lengths_ref, passages_ref, labels_ref, arrived
):
    query_rows = queries_hbm.shape[0]
    copies = [
        pltpu.make_async_copy(passages_hbm, passages_ref, arrived.at[0]),
        pltpu.make_async_copy(lengths_hbm, lengths_ref, arrived.at[1]),
        pltpu.make_async_copy(labels_hbm, labels_ref, arrived.at[2]),
        pltpu.make_async_copy(queries_hbm, payload_ref.at[:query_rows, :], arrived.at[3]),
    ]
    for copy in copies:
        copy.start()
    count, tokens, features = passages_ref.shape
    totals = jnp.zeros((clusters * count, features), F32)
    for copy in copies[:3]:
        copy.wait()
    for p in range(count):
        length = lengths_ref[0:1, p : p + 1]
        document = passages_ref[p]
        wide = document.astype(F32)
        kept = jnp.where(iota((tokens, features), 0) < length, wide, wide[0:1, :])
        masked_ref[p * tokens : (p + 1) * tokens, :] = kept.astype(BF16)
        target = jnp.where(iota((1, tokens), 1) < length, labels_ref[p : p + 1, :] * count + p, -1)
        chosen = (iota((clusters * count, tokens), 0) == target).astype(F32).astype(BF16)
        totals = totals + jnp.dot(chosen, document, preferred_element_type=F32)
    high = totals.astype(BF16).astype(F32)
    payload_ref[query_rows:, :] = jnp.concatenate([high, totals - high], axis=0).astype(BF16)
    copies[3].wait()


def best_rows(document_refs, vectors, count, tokens):
    best, rows = [], count * tokens
    for document_ref in document_refs:
        for at in range(0, document_ref.shape[0], rows):
            scores = rows_dot(document_ref[at : at + rows, :], vectors)
            best += [jnp.max(scores[p * tokens : (p + 1) * tokens, :], axis=0, keepdims=True) for p in range(count)]
    return jnp.concatenate(best, axis=0)


def plain_kernel(count, tokens, query_tokens, query_rows, slots, *refs):
    gathered_refs, document_refs, plain_ref = refs[:slots], refs[slots:-1], refs[-1]
    vectors = jnp.concatenate([slot[:query_rows, :] for slot in gathered_refs], axis=0)
    best = best_rows(document_refs, vectors, count, tokens)
    shape = (plain_ref.shape[0], vectors.shape[0])
    first = iota(shape, 0) * query_tokens
    mean = jnp.where((iota(shape, 1) >= first) & (iota(shape, 1) < first + query_tokens), 1.0 / query_tokens, 0.0)
    plain_ref[...] = rows_dot(mean.astype(F32), best, HIGHEST)


def parts(index, size):
    whole = jnp.floor((index.astype(F32) + 0.5) * (1.0 / size)).astype(I32)
    return whole, index - whole * size


def relative(passage, me, count, bank, columns):
    owner, within = passage // count, passage % count
    column = (owner // bank + columns - me // bank) % columns
    return (column * bank + (owner % bank ^ me % bank)) * count + within


def near_kernel(count, tokens, query_tokens, query_rows, bank, slots, feedback_ref, idf_ref, *refs):
    refs, (plain_ref, near_ref, far_ref, spread_ref, fb_ref, weight_ref) = refs[:-6], refs[-6:]
    plain_kernel(count, tokens, query_tokens, query_rows, len(slots), *refs, plain_ref)
    me = lax.axis_index("shard")
    number, clusters = weight_ref.shape
    each = number // len(slots)
    block, row = parts(iota((1, near_ref.shape[1]), 1), 2 * clusters * count)
    block, column = parts(block, len(slots))
    kind, within = parts(jnp.where(row < clusters * count, row, row - clusters * count), count)
    owner = (bank - 2 * block) % bank
    for s, slot in enumerate(slots):
        owner = jnp.where(column == s, owner + slot * bank, owner)
    place = owner * count + within
    for core, picks_ref in enumerate((near_ref, far_ref)):
        for s, slot in enumerate(slots):
            base = ((me ^ core) % bank + (me // bank + slot) % len(slots) * bank) * each
            fb_ref[s * each : (s + 1) * each, :] = feedback_ref[pl.ds(base, each), :]
            if core == 0:
                weight_ref[s * each : (s + 1) * each, :] = idf_ref[pl.ds(base, each), :].astype(F32) / (8.0 * clusters)
        wanted = relative(fb_ref[...], me, count, bank, len(slots))
        times = jnp.zeros((number, place.shape[1]), F32)
        for k in range(wanted.shape[1]):
            times = times + jnp.where(wanted[:, k : k + 1] == place, 1.0, 0.0)
        for c in range(clusters):
            picks_ref[c * number : (c + 1) * number, :] = jnp.where(kind == c, times, 0.0).astype(BF16)
    shape = (number, clusters * number)
    spread = jnp.zeros(shape, F32)
    for c in range(clusters):
        spread = jnp.where(iota(shape, 1) == iota(shape, 0) + c * number, weight_ref[:, c : c + 1], spread)
    spread_ref[...] = spread


def totals_kernel(skip, *refs):
    slots, totals_ref = refs[:-1], refs[-1]
    rows = totals_ref.shape[0] // len(slots)
    for s, slot in enumerate(slots):
        totals_ref[s * rows : (s + 1) * rows, :] = slot[skip:, :]


def pool_kernel(picks_ref, totals_ref, pooled_ref):
    pooled_ref[...] = jnp.dot(picks_ref[...], totals_ref[...], preferred_element_type=F32)


def expand_kernel(
    count, tokens, places, near_pooled_ref, far_pooled_ref, spread_ref, near_plain_ref, far_plain_ref, *refs
):
    outputs = len(places)
    document_refs, out_refs = refs[:-outputs], refs[-outputs:]
    pooled = near_pooled_ref[...] + far_pooled_ref[...]
    factor = lax.rsqrt(jnp.mean(pooled * pooled, axis=-1, keepdims=True) + 1e-06)
    expansion = (pooled * factor).astype(BF16)
    best = best_rows(document_refs, expansion, count, tokens)
    added = rows_dot(spread_ref[...], best, HIGHEST)
    plain = jnp.concatenate([near_plain_ref[...], far_plain_ref[...]], axis=1)
    both = jnp.concatenate([plain, plain + added], axis=1)
    each = both.shape[0] // outputs
    for place, out_ref in zip(places, out_refs):
        out_ref[...] = both[place * each : (place + 1) * each, :]


def select_kernel(count, bank, places, candidates_ref, *refs):
    block_refs, first_ref, final_ref = [refs[i] for i in places], refs[-2], refs[-1]
    me = lax.axis_index("shard")
    given, wanted = candidates_ref.shape
    width = block_refs[0].shape[1] // 2
    place = relative(candidates_ref[...], me, count, bank, len(places))
    owner, within = place // count % (width // count), place % count
    half = width // 2
    block = (bank - owner // 2 * 2) % bank // 2
    place = place // width * width + owner % 2 * half + block * count + within
    rows, lanes = -(-given // 8) * 8, -(-wanted // 128) * 128
    place = jnp.pad(place, ((0, rows - given), (0, lanes - wanted)))
    for side, out_ref in enumerate((first_ref, final_ref)):
        dense = jnp.concatenate([r[:, side * width : (side + 1) * width] for r in block_refs], axis=1)
        dense = jnp.pad(dense, ((0, rows - given), (0, 0)))
        pieces = []
        for at in range(0, place.shape[1], 128):
            here = place[:, at : at + 128]
            piece = jnp.zeros((rows, 128), F32)
            for group in range(dense.shape[1] // 128):
                found = jnp.take_along_axis(
                    dense[:, group * 128 : (group + 1) * 128], here & 127, axis=1, mode="promise_in_bounds"
                )
                piece = jnp.where((here >> 7) == group, found, piece)
            pieces.append(piece)
        out_ref[...] = jnp.concatenate(pieces, axis=1)[:given, :wanted]


def call(kernel, out_shape, *operands, scratch=(), specs=None, cost=None, vmem=VMEM_BYTES):
    return pl.pallas_call(
        kernel,
        out_shape=out_shape,
        in_specs=specs or [pl.BlockSpec(memory_space=pltpu.VMEM)] * len(operands),
        scratch_shapes=scratch,
        compiler_params=pltpu.CompilerParams(vmem_limit_bytes=vmem),
        cost_estimate=cost,
    )(*operands)


def local(devices, queries, passages, labels, lengths, candidates, feedback, idf):
    passages = lax.all_gather(passages, "rep", axis=0, tiled=True)
    count, tokens, features = passages.shape
    each, query_tokens, _ = queries.shape
    clusters = idf.shape[1]
    bank = min(1 << BANK_BITS, devices)
    columns = devices // bank
    number = columns * each
    query_rows = each * query_tokens
    total_rows = 2 * clusters * count
    sds = jax.ShapeDtypeStruct

    def shift(x, s):
        return lax.ppermute(x, "shard", [(i, (i + s * bank) % devices) for i in range(devices)])

    def swap(x, m):
        return lax.ppermute(x, "shard", [(i, i ^ m) for i in range(devices)])

    payload, masked = call(
        functools.partial(prepare_kernel, clusters),
        (sds((query_rows + total_rows, features), BF16), sds((count * tokens, features), BF16)),
        *[
            pltpu.with_memory_space_constraint(x, pltpu.HBM)
            for x in (lengths.reshape(1, count), queries.reshape(query_rows, features), passages, labels)
        ],
        specs=[pl.BlockSpec(memory_space=pltpu.HBM)] * 4,
        scratch=[
            pltpu.VMEM((1, count), I32),
            pltpu.VMEM((count, tokens, features), BF16),
            pltpu.VMEM((count, tokens), I32),
            pltpu.SemaphoreType.DMA((4,)),
        ],
    )
    slots = [0, columns - 1] + list(range(1, columns - 1))
    gathered = [payload] + [shift(payload, -s) for s in slots[1:]]
    near = [(bank - 2 * b) % bank for b in range(bank // 2)]
    documents = [masked] + [swap(masked, m) for m in near[1:]]
    far_documents = swap(jnp.concatenate(documents, axis=0), 1)
    half = bank * count // 2
    plain = functools.partial(plain_kernel, count, tokens, query_tokens, query_rows, columns)
    picks_shape = sds((clusters * number, bank // 2 * columns * total_rows), BF16)
    ready = call(
        functools.partial(near_kernel, count, tokens, query_tokens, query_rows, bank, slots),
        (sds((number, half), F32), picks_shape, picks_shape, sds((number, clusters * number), F32)),
        feedback,
        idf,
        *gathered,
        *documents,
        scratch=[pltpu.VMEM((number, feedback.shape[1]), I32), pltpu.VMEM((number, clusters), F32)],
    )
    far_plain = call(plain, sds((number, half), F32), *gathered, far_documents)
    own = call(
        functools.partial(totals_kernel, query_rows),
        sds((columns * total_rows, features), BF16),
        *gathered,
        cost=pl.CostEstimate(flops=10**9, bytes_accessed=0, transcendentals=0),
    )
    ready, *others = lax.optimization_barrier((ready, *[swap(own, m) for m in near[1:]]))
    near_plain, near_picks, far_picks, spread = ready
    totals = jnp.concatenate([own, *others], axis=0)
    pooled_shape = sds((clusters * number, features), F32)
    far_pooled = swap(call(pool_kernel, pooled_shape, far_picks, totals, cost=pl.CostEstimate(flops=3 * 10**9, bytes_accessed=0, transcendentals=0)), 1)
    near_pooled = call(pool_kernel, pooled_shape, near_picks, totals)
    returns = list(range(1, columns)) + [0]
    blocks = call(
        functools.partial(expand_kernel, count, tokens, [slots.index(m) for m in returns]),
        [sds((each, 2 * bank * count), F32)] * columns,
        near_pooled,
        far_pooled,
        spread,
        near_plain,
        far_plain,
        *documents,
        far_documents,
    )
    blocks = [shift(block, s) if s else block for s, block in zip(returns, blocks)]
    return call(
        functools.partial(select_kernel, count, bank, [returns.index(-s % columns) for s in range(columns)]),
        (sds(candidates.shape, F32), sds(candidates.shape, F32)),
        candidates,
        *blocks,
    )


def solution(mesh):
    return jax.shard_map(
        functools.partial(local, mesh.shape["shard"]),
        mesh=mesh,
        in_specs=(
            P(("rep", "shard"), None, None),
            P(("shard", "rep"), None, None),
            P("shard", None),
            P("shard"),
            P(("rep", "shard"), None),
            P("rep", None),
            P("rep", None),
        ),
        out_specs=(P(("rep", "shard"), None), P(("rep", "shard"), None)),
        check_vma=False,
    )
```

```python
import functools

import jax
import jax.numpy as jnp
from jax import lax
from jax.experimental import pallas as pl
from jax.experimental.pallas import tpu as pltpu
from jax.sharding import PartitionSpec as P

BANK_BITS = 3
HIGHEST = lax.Precision.HIGHEST
BF16, F32, I32 = jnp.bfloat16, jnp.float32, jnp.int32
VMEM_BYTES = 48 * 1024 * 1024


def iota(shape, dim):
    return lax.broadcasted_iota(I32, shape, dim)


def rows_dot(a, b, precision=None):
    return lax.dot_general(a, b, (((1,), (1,)), ((), ())), precision=precision, preferred_element_type=F32)


def prepare_kernel(
    clusters, lengths_hbm, queries_hbm, passages_hbm, labels_hbm, payload_ref, passages_ref, lengths_ref, labels_ref, arrived
):
    query_rows = queries_hbm.shape[0]
    copies = [
        pltpu.make_async_copy(passages_hbm, passages_ref, arrived.at[0]),
        pltpu.make_async_copy(lengths_hbm, lengths_ref, arrived.at[1]),
        pltpu.make_async_copy(labels_hbm, labels_ref, arrived.at[2]),
        pltpu.make_async_copy(queries_hbm, payload_ref.at[:query_rows, :], arrived.at[3]),
    ]
    for copy in copies:
        copy.start()
    count, tokens, features = passages_ref.shape
    for copy in copies[1:3]:
        copy.wait()
    chosen = []
    for p in range(count):
        target = jnp.where(iota((1, tokens), 1) < lengths_ref[0:1, p : p + 1], labels_ref[p : p + 1, :] * count + p, -1)
        chosen.append((iota((clusters * count, tokens), 0) == target).astype(F32).astype(BF16))
    copies[0].wait()
    totals = jnp.zeros((clusters * count, features), F32)
    for p in range(count):
        totals = totals + jnp.dot(chosen[p], passages_ref[p], preferred_element_type=F32)
    high = totals.astype(BF16).astype(F32)
    payload_ref[query_rows:, :] = jnp.concatenate([high, totals - high], axis=0).astype(BF16)
    copies[3].wait()


def mask_kernel(passages_ref, lengths_ref, masked_ref):
    count, tokens, features = passages_ref.shape
    for p in range(count):
        wide = passages_ref[p].astype(F32)
        kept = jnp.where(iota((tokens, features), 0) < lengths_ref[0:1, p : p + 1], wide, wide[0:1, :])
        masked_ref[p * tokens : (p + 1) * tokens, :] = kept.astype(BF16)


def best_rows(document_refs, vectors, count, tokens):
    best, rows = [], count * tokens
    for document_ref in document_refs:
        for at in range(0, document_ref.shape[0], rows):
            scores = rows_dot(document_ref[at : at + rows, :], vectors)
            best += [jnp.max(scores[p * tokens : (p + 1) * tokens, :], axis=0, keepdims=True) for p in range(count)]
    return jnp.concatenate(best, axis=0)


def plain_kernel(count, tokens, query_tokens, query_rows, slots, *refs):
    gathered_refs, document_refs, plain_ref = refs[:slots], refs[slots:-1], refs[-1]
    vectors = jnp.concatenate([slot[:query_rows, :] for slot in gathered_refs], axis=0)
    best = best_rows(document_refs, vectors, count, tokens)
    shape = (plain_ref.shape[0], vectors.shape[0])
    first = iota(shape, 0) * query_tokens
    mean = jnp.where((iota(shape, 1) >= first) & (iota(shape, 1) < first + query_tokens), 1.0 / query_tokens, 0.0)
    plain_ref[...] = rows_dot(mean.astype(F32), best, HIGHEST)


def parts(index, size):
    whole = jnp.floor((index.astype(F32) + 0.5) * (1.0 / size)).astype(I32)
    return whole, index - whole * size


def relative(passage, me, count, bank, columns):
    owner, within = passage // count, passage % count
    column = (owner // bank + columns - me // bank) % columns
    return (column * bank + (owner % bank ^ me % bank)) * count + within


def near_kernel(count, tokens, query_tokens, query_rows, bank, slots, feedback_ref, idf_ref, *refs):
    refs, (plain_ref, near_ref, far_ref, spread_ref, fb_ref, weight_ref) = refs[:-6], refs[-6:]
    plain_kernel(count, tokens, query_tokens, query_rows, len(slots), *refs, plain_ref)
    me = lax.axis_index("shard")
    number, clusters = weight_ref.shape
    each = number // len(slots)
    block, row = parts(iota((1, near_ref.shape[1]), 1), 2 * clusters * count)
    block, column = parts(block, len(slots))
    kind, within = parts(jnp.where(row < clusters * count, row, row - clusters * count), count)
    owner = (bank - 2 * block) % bank
    for s, slot in enumerate(slots):
        owner = jnp.where(column == s, owner + slot * bank, owner)
    place = owner * count + within
    for core, picks_ref in enumerate((near_ref, far_ref)):
        for s, slot in enumerate(slots):
            base = ((me ^ core) % bank + (me // bank + slot) % len(slots) * bank) * each
            fb_ref[s * each : (s + 1) * each, :] = feedback_ref[pl.ds(base, each), :]
            if core == 0:
                weight_ref[s * each : (s + 1) * each, :] = idf_ref[pl.ds(base, each), :].astype(F32) / (8.0 * clusters)
        wanted = relative(fb_ref[...], me, count, bank, len(slots))
        times = jnp.zeros((number, place.shape[1]), F32)
        for k in range(wanted.shape[1]):
            times = times + jnp.where(wanted[:, k : k + 1] == place, 1.0, 0.0)
        for c in range(clusters):
            picks_ref[c * number : (c + 1) * number, :] = jnp.where(kind == c, times, 0.0).astype(BF16)
    shape = (number, clusters * number)
    spread = jnp.zeros(shape, F32)
    for c in range(clusters):
        spread = jnp.where(iota(shape, 1) == iota(shape, 0) + c * number, weight_ref[:, c : c + 1], spread)
    spread_ref[...] = spread


def totals_kernel(skip, *refs):
    slots, totals_ref = refs[:-1], refs[-1]
    rows = totals_ref.shape[0] // len(slots)
    for s, slot in enumerate(slots):
        totals_ref[s * rows : (s + 1) * rows, :] = slot[skip:, :]


def pool_kernel(picks_ref, totals_ref, pooled_ref):
    pooled_ref[...] = jnp.dot(picks_ref[...], totals_ref[...], preferred_element_type=F32)


def expand_kernel(
    count, tokens, places, near_pooled_ref, far_pooled_ref, spread_ref, near_plain_ref, far_plain_ref, *refs
):
    outputs = len(places)
    document_refs, out_refs = refs[:-outputs], refs[-outputs:]
    pooled = near_pooled_ref[...] + far_pooled_ref[...]
    factor = lax.rsqrt(jnp.mean(pooled * pooled, axis=-1, keepdims=True) + 1e-06)
    expansion = (pooled * factor).astype(BF16)
    best = best_rows(document_refs, expansion, count, tokens)
    added = rows_dot(spread_ref[...], best, HIGHEST)
    plain = jnp.concatenate([near_plain_ref[...], far_plain_ref[...]], axis=1)
    both = jnp.concatenate([plain, plain + added], axis=1)
    each = both.shape[0] // outputs
    for place, out_ref in zip(places, out_refs):
        out_ref[...] = both[place * each : (place + 1) * each, :]


def select_kernel(count, bank, places, candidates_ref, *refs):
    block_refs, first_ref, final_ref = [refs[i] for i in places], refs[-2], refs[-1]
    me = lax.axis_index("shard")
    given, wanted = candidates_ref.shape
    width = block_refs[0].shape[1] // 2
    place = relative(candidates_ref[...], me, count, bank, len(places))
    owner, within = place // count % (width // count), place % count
    half = width // 2
    block = (bank - owner // 2 * 2) % bank // 2
    place = place // width * width + owner % 2 * half + block * count + within
    rows, lanes = -(-given // 8) * 8, -(-wanted // 128) * 128
    place = jnp.pad(place, ((0, rows - given), (0, lanes - wanted)))
    for side, out_ref in enumerate((first_ref, final_ref)):
        dense = jnp.concatenate([r[:, side * width : (side + 1) * width] for r in block_refs], axis=1)
        dense = jnp.pad(dense, ((0, rows - given), (0, 0)))
        pieces = []
        for at in range(0, place.shape[1], 128):
            here = place[:, at : at + 128]
            piece = jnp.zeros((rows, 128), F32)
            for group in range(dense.shape[1] // 128):
                found = jnp.take_along_axis(
                    dense[:, group * 128 : (group + 1) * 128], here & 127, axis=1, mode="promise_in_bounds"
                )
                piece = jnp.where((here >> 7) == group, found, piece)
            pieces.append(piece)
        out_ref[...] = jnp.concatenate(pieces, axis=1)[:given, :wanted]


def call(kernel, out_shape, *operands, scratch=(), specs=None, cost=None, vmem=VMEM_BYTES):
    return pl.pallas_call(
        kernel,
        out_shape=out_shape,
        in_specs=specs or [pl.BlockSpec(memory_space=pltpu.VMEM)] * len(operands),
        scratch_shapes=scratch,
        compiler_params=pltpu.CompilerParams(vmem_limit_bytes=vmem),
        cost_estimate=cost,
    )(*operands)


def local(devices, queries, passages, labels, lengths, candidates, feedback, idf):
    passages = lax.all_gather(passages, "rep", axis=0, tiled=True)
    count, tokens, features = passages.shape
    each, query_tokens, _ = queries.shape
    clusters = idf.shape[1]
    bank = min(1 << BANK_BITS, devices)
    columns = devices // bank
    number = columns * each
    query_rows = each * query_tokens
    total_rows = 2 * clusters * count
    sds = jax.ShapeDtypeStruct

    def shift(x, s):
        return lax.ppermute(x, "shard", [(i, (i + s * bank) % devices) for i in range(devices)])

    def swap(x, m):
        return lax.ppermute(x, "shard", [(i, i ^ m) for i in range(devices)])

    payload, loaded, ends = call(
        functools.partial(prepare_kernel, clusters),
        (
            sds((query_rows + total_rows, features), BF16),
            sds((count, tokens, features), BF16),
            sds((1, count), I32),
        ),
        *[
            pltpu.with_memory_space_constraint(x, pltpu.HBM)
            for x in (lengths.reshape(1, count), queries.reshape(query_rows, features), passages, labels)
        ],
        specs=[pl.BlockSpec(memory_space=pltpu.HBM)] * 4,
        scratch=[pltpu.VMEM((count, tokens), I32), pltpu.SemaphoreType.DMA((4,))],
    )
    masked = call(mask_kernel, sds((count * tokens, features), BF16), loaded, ends)
    slots = [0, columns - 1] + list(range(1, columns - 1))
    gathered = [payload] + [shift(payload, -s) for s in slots[1:]]
    near = [(bank - 2 * b) % bank for b in range(bank // 2)]
    documents = [masked] + [swap(masked, m) for m in near[1:]]
    far_documents = swap(jnp.concatenate(documents, axis=0), 1)
    half = bank * count // 2
    plain = functools.partial(plain_kernel, count, tokens, query_tokens, query_rows, columns)
    picks_shape = sds((clusters * number, bank // 2 * columns * total_rows), BF16)
    ready = call(
        functools.partial(near_kernel, count, tokens, query_tokens, query_rows, bank, slots),
        (sds((number, half), F32), picks_shape, picks_shape, sds((number, clusters * number), F32)),
        feedback,
        idf,
        *gathered,
        *documents,
        scratch=[pltpu.VMEM((number, feedback.shape[1]), I32), pltpu.VMEM((number, clusters), F32)],
    )
    far_plain = call(plain, sds((number, half), F32), *gathered, far_documents)
    own = call(
        functools.partial(totals_kernel, query_rows),
        sds((columns * total_rows, features), BF16),
        *gathered,
        cost=pl.CostEstimate(flops=10**9, bytes_accessed=0, transcendentals=0),
    )
    ready, *others = lax.optimization_barrier((ready, *[swap(own, m) for m in near[1:]]))
    near_plain, near_picks, far_picks, spread = ready
    totals = jnp.concatenate([own, *others], axis=0)
    pooled_shape = sds((clusters * number, features), F32)
    far_pooled = swap(call(pool_kernel, pooled_shape, far_picks, totals, cost=pl.CostEstimate(flops=3 * 10**9, bytes_accessed=0, transcendentals=0)), 1)
    near_pooled = call(pool_kernel, pooled_shape, near_picks, totals)
    returns = list(range(1, columns)) + [0]
    blocks = call(
        functools.partial(expand_kernel, count, tokens, [slots.index(m) for m in returns]),
        [sds((each, 2 * bank * count), F32)] * columns,
        near_pooled,
        far_pooled,
        spread,
        near_plain,
        far_plain,
        *documents,
        far_documents,
    )
    blocks = [shift(block, s) if s else block for s, block in zip(returns, blocks)]
    return call(
        functools.partial(select_kernel, count, bank, [returns.index(-s % columns) for s in range(columns)]),
        (sds(candidates.shape, F32), sds(candidates.shape, F32)),
        candidates,
        *blocks,
    )


def solution(mesh):
    return jax.shard_map(
        functools.partial(local, mesh.shape["shard"]),
        mesh=mesh,
        in_specs=(
            P(("rep", "shard"), None, None),
            P(("shard", "rep"), None, None),
            P("shard", None),
            P("shard"),
            P(("rep", "shard"), None),
            P("rep", None),
            P("rep", None),
        ),
        out_specs=(P(("rep", "shard"), None), P(("rep", "shard"), None)),
        check_vma=False,
    )
```

```python
import functools

import jax
import jax.numpy as jnp
from jax import lax
from jax.experimental import pallas as pl
from jax.experimental.pallas import tpu as pltpu
from jax.sharding import PartitionSpec as P

BANK_BITS = 3
HIGHEST = lax.Precision.HIGHEST
BF16, F32, I32 = jnp.bfloat16, jnp.float32, jnp.int32
VMEM_BYTES = 48 * 1024 * 1024


def iota(shape, dim):
    return lax.broadcasted_iota(I32, shape, dim)


def rows_dot(a, b, precision=None):
    return lax.dot_general(a, b, (((1,), (1,)), ((), ())), precision=precision, preferred_element_type=F32)


def prepare_kernel(
    clusters, lengths_hbm, queries_hbm, passages_hbm, labels_hbm, payload_ref, masked_ref, lengths_ref, passages_ref, labels_ref, arrived
):
    query_rows = queries_hbm.shape[0]
    copies = [
        pltpu.make_async_copy(passages_hbm, passages_ref, arrived.at[0]),
        pltpu.make_async_copy(lengths_hbm, lengths_ref, arrived.at[1]),
        pltpu.make_async_copy(labels_hbm, labels_ref, arrived.at[2]),
        pltpu.make_async_copy(queries_hbm, payload_ref.at[:query_rows, :], arrived.at[3]),
    ]
    for copy in copies:
        copy.start()
    count, tokens, features = passages_ref.shape
    totals = jnp.zeros((clusters * count, features), F32)
    for copy in copies[:3]:
        copy.wait()
    for p in range(count):
        length = lengths_ref[0:1, p : p + 1]
        document = passages_ref[p]
        wide = document.astype(F32)
        kept = jnp.where(iota((tokens, features), 0) < length, wide, wide[0:1, :])
        masked_ref[p * tokens : (p + 1) * tokens, :] = kept.astype(BF16)
        target = jnp.where(iota((1, tokens), 1) < length, labels_ref[p : p + 1, :] * count + p, -1)
        chosen = (iota((clusters * count, tokens), 0) == target).astype(F32).astype(BF16)
        totals = totals + jnp.dot(chosen, document, preferred_element_type=F32)
    high = totals.astype(BF16).astype(F32)
    payload_ref[query_rows:, :] = jnp.concatenate([high, totals - high], axis=0).astype(BF16)
    copies[3].wait()


def best_rows(document_refs, vectors, count, tokens):
    best, rows = [], count * tokens
    for document_ref in document_refs:
        for at in range(0, document_ref.shape[0], rows):
            scores = rows_dot(document_ref[at : at + rows, :], vectors)
            best += [jnp.max(scores[p * tokens : (p + 1) * tokens, :], axis=0, keepdims=True) for p in range(count)]
    return jnp.concatenate(best, axis=0)


def plain_kernel(count, tokens, query_tokens, query_rows, slots, *refs):
    gathered_refs, document_refs, plain_ref = refs[:slots], refs[slots:-1], refs[-1]
    vectors = jnp.concatenate([slot[:query_rows, :] for slot in gathered_refs], axis=0)
    best = best_rows(document_refs, vectors, count, tokens)
    shape = (plain_ref.shape[0], vectors.shape[0])
    first = iota(shape, 0) * query_tokens
    mean = jnp.where((iota(shape, 1) >= first) & (iota(shape, 1) < first + query_tokens), 1.0 / query_tokens, 0.0)
    plain_ref[...] = rows_dot(mean.astype(F32), best, HIGHEST)


def parts(index, size):
    whole = jnp.floor((index.astype(F32) + 0.5) * (1.0 / size)).astype(I32)
    return whole, index - whole * size


def relative(passage, me, count, bank, columns):
    owner, within = passage // count, passage % count
    column = (owner // bank + columns - me // bank) % columns
    return (column * bank + (owner % bank ^ me % bank)) * count + within


def near_kernel(count, tokens, query_tokens, query_rows, bank, slots, feedback_ref, idf_ref, *refs):
    refs, (plain_ref, near_ref, far_ref, spread_ref, fb_ref, weight_ref) = refs[:-6], refs[-6:]
    plain_kernel(count, tokens, query_tokens, query_rows, len(slots), *refs, plain_ref)
    me = lax.axis_index("shard")
    number, clusters = weight_ref.shape
    each = number // len(slots)
    block, row = parts(iota((1, near_ref.shape[1]), 1), 2 * clusters * count)
    block, column = parts(block, len(slots))
    kind, within = parts(jnp.where(row < clusters * count, row, row - clusters * count), count)
    owner = (bank - 2 * block) % bank
    for s, slot in enumerate(slots):
        owner = jnp.where(column == s, owner + slot * bank, owner)
    place = owner * count + within
    for core, picks_ref in enumerate((near_ref, far_ref)):
        for s, slot in enumerate(slots):
            base = ((me ^ core) % bank + (me // bank + slot) % len(slots) * bank) * each
            fb_ref[s * each : (s + 1) * each, :] = feedback_ref[pl.ds(base, each), :]
            if core == 0:
                weight_ref[s * each : (s + 1) * each, :] = idf_ref[pl.ds(base, each), :].astype(F32) / (8.0 * clusters)
        wanted = relative(fb_ref[...], me, count, bank, len(slots))
        times = jnp.zeros((number, place.shape[1]), F32)
        for k in range(wanted.shape[1]):
            times = times + jnp.where(wanted[:, k : k + 1] == place, 1.0, 0.0)
        for c in range(clusters):
            picks_ref[c * number : (c + 1) * number, :] = jnp.where(kind == c, times, 0.0).astype(BF16)
    shape = (number, clusters * number)
    spread = jnp.zeros(shape, F32)
    for c in range(clusters):
        spread = jnp.where(iota(shape, 1) == iota(shape, 0) + c * number, weight_ref[:, c : c + 1], spread)
    spread_ref[...] = spread


def totals_kernel(skip, *refs):
    slots, totals_ref = refs[:-1], refs[-1]
    rows = totals_ref.shape[0] // len(slots)
    for s, slot in enumerate(slots):
        totals_ref[s * rows : (s + 1) * rows, :] = slot[skip:, :]


def pool_kernel(picks_ref, totals_ref, pooled_ref):
    pooled_ref[...] = jnp.dot(picks_ref[...], totals_ref[...], preferred_element_type=F32)


def expand_kernel(
    count, tokens, places, near_pooled_ref, far_pooled_ref, spread_ref, near_plain_ref, far_plain_ref, *refs
):
    outputs = len(places)
    document_refs, out_refs = refs[:-outputs], refs[-outputs:]
    pooled = near_pooled_ref[...] + far_pooled_ref[...]
    factor = lax.rsqrt(jnp.mean(pooled * pooled, axis=-1, keepdims=True) + 1e-06)
    expansion = (pooled * factor).astype(BF16)
    best = best_rows(document_refs, expansion, count, tokens)
    added = rows_dot(spread_ref[...], best, HIGHEST)
    plain = jnp.concatenate([near_plain_ref[...], far_plain_ref[...]], axis=1)
    both = jnp.concatenate([plain, plain + added], axis=1)
    each = both.shape[0] // outputs
    for place, out_ref in zip(places, out_refs):
        out_ref[...] = both[place * each : (place + 1) * each, :]


def place_kernel(count, bank, columns, candidates_ref, place_ref):
    me = lax.axis_index("shard")
    given, wanted = candidates_ref.shape
    width = bank * count
    place = relative(candidates_ref[...], me, count, bank, columns)
    owner, within = place // count % bank, place % count
    block = (bank - owner // 2 * 2) % bank // 2
    place = place // width * width + owner % 2 * (width // 2) + block * count + within
    rows, lanes = place_ref.shape
    place_ref[...] = jnp.pad(place, ((0, rows - given), (0, lanes - wanted)))


def select_kernel(places, place_ref, *refs):
    block_refs, first_ref, final_ref = [refs[i] for i in places], refs[-2], refs[-1]
    given, wanted = first_ref.shape
    width = block_refs[0].shape[1] // 2
    place = place_ref[...]
    rows = place.shape[0]
    for side, out_ref in enumerate((first_ref, final_ref)):
        dense = jnp.concatenate([r[:, side * width : (side + 1) * width] for r in block_refs], axis=1)
        dense = jnp.pad(dense, ((0, rows - given), (0, 0)))
        pieces = []
        for at in range(0, place.shape[1], 128):
            here = place[:, at : at + 128]
            piece = jnp.zeros((rows, 128), F32)
            for group in range(dense.shape[1] // 128):
                found = jnp.take_along_axis(
                    dense[:, group * 128 : (group + 1) * 128], here & 127, axis=1, mode="promise_in_bounds"
                )
                piece = jnp.where((here >> 7) == group, found, piece)
            pieces.append(piece)
        out_ref[...] = jnp.concatenate(pieces, axis=1)[:given, :wanted]


def call(kernel, out_shape, *operands, scratch=(), specs=None, cost=None, vmem=VMEM_BYTES):
    return pl.pallas_call(
        kernel,
        out_shape=out_shape,
        in_specs=specs or [pl.BlockSpec(memory_space=pltpu.VMEM)] * len(operands),
        scratch_shapes=scratch,
        compiler_params=pltpu.CompilerParams(vmem_limit_bytes=vmem),
        cost_estimate=cost,
    )(*operands)


def local(devices, queries, passages, labels, lengths, candidates, feedback, idf):
    passages = lax.all_gather(passages, "rep", axis=0, tiled=True)
    count, tokens, features = passages.shape
    each, query_tokens, _ = queries.shape
    clusters = idf.shape[1]
    bank = min(1 << BANK_BITS, devices)
    columns = devices // bank
    number = columns * each
    query_rows = each * query_tokens
    total_rows = 2 * clusters * count
    sds = jax.ShapeDtypeStruct

    def shift(x, s):
        return lax.ppermute(x, "shard", [(i, (i + s * bank) % devices) for i in range(devices)])

    def swap(x, m):
        return lax.ppermute(x, "shard", [(i, i ^ m) for i in range(devices)])

    payload, masked = call(
        functools.partial(prepare_kernel, clusters),
        (sds((query_rows + total_rows, features), BF16), sds((count * tokens, features), BF16)),
        *[
            pltpu.with_memory_space_constraint(x, pltpu.HBM)
            for x in (lengths.reshape(1, count), queries.reshape(query_rows, features), passages, labels)
        ],
        specs=[pl.BlockSpec(memory_space=pltpu.HBM)] * 4,
        scratch=[
            pltpu.VMEM((1, count), I32),
            pltpu.VMEM((count, tokens, features), BF16),
            pltpu.VMEM((count, tokens), I32),
            pltpu.SemaphoreType.DMA((4,)),
        ],
    )
    slots = [0, columns - 1] + list(range(1, columns - 1))
    gathered = [payload] + [shift(payload, -s) for s in slots[1:]]
    near = [(bank - 2 * b) % bank for b in range(bank // 2)]
    documents = [masked] + [swap(masked, m) for m in near[1:]]
    far_documents = swap(jnp.concatenate(documents, axis=0), 1)
    half = bank * count // 2
    plain = functools.partial(plain_kernel, count, tokens, query_tokens, query_rows, columns)
    picks_shape = sds((clusters * number, bank // 2 * columns * total_rows), BF16)
    ready = call(
        functools.partial(near_kernel, count, tokens, query_tokens, query_rows, bank, slots),
        (sds((number, half), F32), picks_shape, picks_shape, sds((number, clusters * number), F32)),
        feedback,
        idf,
        *gathered,
        *documents,
        scratch=[pltpu.VMEM((number, feedback.shape[1]), I32), pltpu.VMEM((number, clusters), F32)],
    )
    far_plain = call(plain, sds((number, half), F32), *gathered, far_documents)
    own = call(
        functools.partial(totals_kernel, query_rows),
        sds((columns * total_rows, features), BF16),
        *gathered,
        cost=pl.CostEstimate(flops=10**9, bytes_accessed=0, transcendentals=0),
    )
    ready, *others = lax.optimization_barrier((ready, *[swap(own, m) for m in near[1:]]))
    near_plain, near_picks, far_picks, spread = ready
    totals = jnp.concatenate([own, *others], axis=0)
    pooled_shape = sds((clusters * number, features), F32)
    far_pooled = swap(call(pool_kernel, pooled_shape, far_picks, totals, cost=pl.CostEstimate(flops=3 * 10**9, bytes_accessed=0, transcendentals=0)), 1)
    near_pooled = call(pool_kernel, pooled_shape, near_picks, totals)
    returns = list(range(1, columns)) + [0]
    blocks = call(
        functools.partial(expand_kernel, count, tokens, [slots.index(m) for m in returns]),
        [sds((each, 2 * bank * count), F32)] * columns,
        near_pooled,
        far_pooled,
        spread,
        near_plain,
        far_plain,
        *documents,
        far_documents,
    )
    blocks = [shift(block, s) if s else block for s, block in zip(returns, blocks)]
    rows, lanes = -(-each // 8) * 8, -(-candidates.shape[1] // 128) * 128
    place = call(functools.partial(place_kernel, count, bank, columns), sds((rows, lanes), I32), candidates)
    return call(
        functools.partial(select_kernel, [returns.index(-s % columns) for s in range(columns)]),
        (sds(candidates.shape, F32), sds(candidates.shape, F32)),
        place,
        *blocks,
    )


def solution(mesh):
    return jax.shard_map(
        functools.partial(local, mesh.shape["shard"]),
        mesh=mesh,
        in_specs=(
            P(("rep", "shard"), None, None),
            P(("shard", "rep"), None, None),
            P("shard", None),
            P("shard"),
            P(("rep", "shard"), None),
            P("rep", None),
            P("rep", None),
        ),
        out_specs=(P(("rep", "shard"), None), P(("rep", "shard"), None)),
        check_vma=False,
    )
```
